256 devices in a mesh: segment: 4 (over z_hi, core), expert: 64 (over y, x, z_lo).
Axes of the slice: x: 4, y: 4, z: 8 (z_hi: 2, z_lo: 4; z = z_hi * 4 + z_lo), core: 2. Of those that a mesh axis runs over, the one named last changes fastest.
Arguments:
- x_fwd: bfloat16 [512, 7168], P(('segment', 'expert')), may hold values from -6 to 6
- ids_fwd: int32 [512, 4], P('segment'), may hold values from 0 to 7, all different within a row; in each aligned block of 2 rows (0 to 1, 2 to 3, ...) at most 2 rows name the same one
- probs_fwd: bfloat16 [512, 4], P('segment'), may hold values from 0.049804688 to 0.44921875
- x_bwd: bfloat16 [512, 7168], P(('segment', 'expert')), may hold values from -6 to 6
- ids_bwd: int32 [512, 4], P('segment'), may hold values from 0 to 7, all different within a row; in each aligned block of 2 rows (0 to 1, 2 to 3, ...) at most 2 rows name the same one
- probs_bwd: bfloat16 [512, 4], P('segment'), may hold values from 0.049804688 to 0.44921875
- grad_out: bfloat16 [512, 7168], P(('segment', 'expert')), may hold values from -6 to 6
- w_gate: bfloat16 [4, 7168, 16384], P('segment', None, 'expert'), may hold values from -0.0625 to 0.0625
- w_up: bfloat16 [4, 7168, 16384], P('segment', None, 'expert'), may hold values from -0.0625 to 0.0625
- w_down: bfloat16 [4, 16384, 7168], P('segment', 'expert'), may hold values from -0.125 to 0.125
Outputs:
- fwd_next: bfloat16 [512, 7168], P(('segment', 'expert'))
- bwd_next: bfloat16 [512, 7168], P(('segment', 'expert'))
- dprob: float32 [512, 4], P(('segment', 'expert'))
The draws below stay inside these ranges and needn't reach their ends.
Inputs may be any that keep to these rules, and one draw needn't show every extreme that they name: `ids_fwd`: in each aligned block of 2 rows (the tokens of one device) a row names 4 distinct experts and no expert is named by more than 2 rows; some block reaches 2. The same holds for ids_bwd. `ids_bwd`: as for ids_fwd.
All inputs are finite; a program needn't handle non-finite values.
Results may differ from the reference program's by a relative error of at most 0.0038.
Values may be sent and summed in bfloat16 or wider, within the bound.
No kernel may reach another device: no remote copies, remote signals or barrier semaphores. Data moves between devices by JAX's collectives and lax.ppermute only.
A program may use at most 128 MiB of HBM per device.

```python
import math
import jax
import jax.numpy as jnp
import numpy as np

D = 7168
FF = 2048
EXP_WIN = 8
TOPK_WIN = 4
TOK_DEV = 2
CAP_SRC = 2
SEGMENT_TOK = 128
ALL_TOK = 512
N_SEGMENT = 4


def steps_of(key, shape, split, smallest, top_value):
    level, own = 1.0, jax.random.fold_in(key, 6)
    for axis_at, parts in split:
        draws = jnp.exp(jax.random.uniform(jax.random.fold_in(own, axis_at), (parts,), jnp.float32, smallest / len(split), top_value / len(split)))
        level = level * jnp.repeat(draws, shape[axis_at] // parts).reshape([-1 if axis == axis_at else 1 for axis in range(len(shape))])
    return level


def deal_out(key, own, number, rows, amount, top, bound, lean):
    order = jax.random.permutation(key, amount)
    heavy_load, common = shares(amount, rows * top, bound, lean, True), shares(amount, rows * top, bound, lean, False)
    places = jnp.arange(amount)

    def named(tallies, offset_by):
        used = int((tallies > 0).sum())
        fixed = max(1, used // 4)
        shifted = fixed + (places - fixed + offset_by * (used - fixed)) % max(1, amount - fixed)
        return jnp.zeros((amount,), jnp.int32).at[order[jnp.where(places < fixed, places, shifted)]].set(jnp.asarray(tallies, jnp.int32))

    tallies = jnp.where(number % 4 == 0, named(heavy_load, number // 4), named(common, number - number // 4 - 1))
    mixed = jax.random.permutation(jax.random.fold_in(own, 3), amount)
    donor, sink = mixed[0:amount // 2 * 2:2], mixed[1:amount // 2 * 2:2]
    room = jnp.minimum(tallies[donor] - 1, bound - tallies[sink]) // 2
    room = jnp.where((donor == order[0]) | (sink == order[0]) | (tallies[sink] == 0), 0, jnp.maximum(room, 0))
    shifted = jax.random.randint(jax.random.fold_in(own, 4), (amount // 2,), 0, 1 << 20) % (room + 1)
    tallies = tallies.at[donor].add(-shifted).at[sink].add(shifted)
    members = jnp.searchsorted(jnp.cumsum(tallies), jnp.arange(rows * top), side="right").astype(jnp.int32)
    listing = members.reshape(top, rows).T
    listing = listing[jax.random.permutation(jax.random.fold_in(own, 1), rows)]
    offset_by = jax.random.randint(jax.random.fold_in(own, 2), (rows, 1), 0, top)
    return jnp.take_along_axis(listing, (jnp.arange(top)[None, :] + offset_by) % top, axis=1)


def shares(number_of, total, bound, slope, full):
    portions = [(1 << 20) // math.isqrt(standing ** slope) + 1 for standing in range(1, number_of + 1)]
    largest = bound if full else min(bound, max(-(-total // number_of), total * portions[0] // sum(portions)))
    least = 1 if total - largest >= number_of - 1 else 0
    counts, surplus = [largest] + [least] * (number_of - 1), total - largest - least * (number_of - 1)
    while surplus > 0:
        free = [i for i in range(1, number_of) if counts[i] < largest] or [i for i in range(1, number_of) if counts[i] < bound]
        pool, remaining = sum([portions[i] for i in free]), surplus
        for i in free:
            addition = min(bound - counts[i], max(1, remaining * portions[i] // pool), surplus)
            counts[i] = counts[i] + addition
            surplus = surplus - addition
    return np.array(counts)


def noise(own_key, shape, width, bound, split=(), held_as=jnp.bfloat16):
    entries = width * jax.random.normal(own_key, shape, jnp.float32)
    if split:
        entries = entries * steps_of(own_key, shape, split, -0.22, 0.18)
    return jnp.clip(entries, -bound, bound).astype(held_as)


def setup_inputs(seed: int = 0) -> dict:
    key_of = jax.random.split(jax.random.key(seed), 11)
    x_fwd = noise(key_of[0], (ALL_TOK, D), 1.0, 6.0, ((0, 256),))
    ids_fwd_keys = jax.random.split(jax.random.fold_in(key_of[1], 1), ALL_TOK // TOK_DEV)
    ids_fwd_turns = jax.random.permutation(jax.random.fold_in(key_of[1], 3), ALL_TOK // TOK_DEV)
    ids_fwd = jax.vmap(lambda own, number: deal_out(jax.random.fold_in(key_of[1], 2), own, number, TOK_DEV, EXP_WIN, TOPK_WIN, CAP_SRC, 2))(ids_fwd_keys, ids_fwd_turns).reshape((ALL_TOK, TOPK_WIN))
    probs_fwd = jnp.clip(0.049804688 + 0.39941406 * jax.random.uniform(key_of[2], (ALL_TOK, TOPK_WIN), jnp.float32) ** steps_of(key_of[2], (ALL_TOK, TOPK_WIN), ((0, 4),), -0.2, 0.2), 0.049804688, 0.44921875).astype(jnp.bfloat16)
    x_bwd = noise(key_of[3], (ALL_TOK, D), 1.0, 6.0, ((0, 256),))
    ids_bwd_keys = jax.random.split(jax.random.fold_in(key_of[4], 1), ALL_TOK // TOK_DEV)
    ids_bwd_turns = jax.random.permutation(jax.random.fold_in(key_of[4], 3), ALL_TOK // TOK_DEV)
    ids_bwd = jax.vmap(lambda own, number: deal_out(jax.random.fold_in(key_of[4], 2), own, number, TOK_DEV, EXP_WIN, TOPK_WIN, CAP_SRC, 2))(ids_bwd_keys, ids_bwd_turns).reshape((ALL_TOK, TOPK_WIN))
    probs_bwd = jnp.clip(0.049804688 + 0.39941406 * jax.random.uniform(key_of[5], (ALL_TOK, TOPK_WIN), jnp.float32) ** steps_of(key_of[5], (ALL_TOK, TOPK_WIN), ((0, 4),), -0.2, 0.2), 0.049804688, 0.44921875).astype(jnp.bfloat16)
    grad_out = noise(key_of[6], (ALL_TOK, D), 1.0, 6.0, ((0, 256),))
    w_gate = noise(key_of[7], (N_SEGMENT, D, EXP_WIN * FF), D ** -0.5, 0.0625, ((0, 4), (2, 64)))
    w_up = noise(key_of[8], (N_SEGMENT, D, EXP_WIN * FF), D ** -0.5, 0.0625, ((0, 4), (2, 64)))
    w_down = noise(key_of[9], (N_SEGMENT, EXP_WIN * FF, D), FF ** -0.5, 0.125, ((0, 4), (1, 64)))
    return {"x_fwd": x_fwd, "ids_fwd": ids_fwd, "probs_fwd": probs_fwd, "x_bwd": x_bwd, "ids_bwd": ids_bwd, "probs_bwd": probs_bwd, "grad_out": grad_out, "w_gate": w_gate, "w_up": w_up, "w_down": w_down}


def gate_weights(ids, probs, expert):
    return jnp.sum(jnp.where(ids == expert, probs.astype(jnp.float32), 0.0), axis=-1)


def reference(x_fwd, ids_fwd, probs_fwd, x_bwd, ids_bwd, probs_bwd, grad_out, w_gate, w_up, w_down):
    outputs = []
    grads = []
    dprobs = []
    for segment in range(N_SEGMENT):
        first = segment * SEGMENT_TOK
        x_now = x_fwd[first:first + SEGMENT_TOK]
        xb_now = x_bwd[first:first + SEGMENT_TOK]
        grad_now = grad_out[first:first + SEGMENT_TOK]
        idf = ids_fwd[first:first + SEGMENT_TOK]
        idb = ids_bwd[first:first + SEGMENT_TOK]
        prf = probs_fwd[first:first + SEGMENT_TOK]
        prb = probs_bwd[first:first + SEGMENT_TOK]
        grad_f32 = grad_now.astype(jnp.float32)
        moe_sum = jnp.zeros((SEGMENT_TOK, D), jnp.float32)
        grad_sum = jnp.zeros((SEGMENT_TOK, D), jnp.float32)
        dprob_now = jnp.zeros((SEGMENT_TOK, TOPK_WIN), jnp.float32)
        for expert in range(EXP_WIN):
            w_g = w_gate[segment][:, expert * FF:(expert + 1) * FF]
            w_u = w_up[segment][:, expert * FF:(expert + 1) * FF]
            w_d = w_down[segment][expert * FF:(expert + 1) * FF]
            gate_act = jnp.dot(x_now, w_g, preferred_element_type=jnp.float32)
            up_act = jnp.dot(x_now, w_u, preferred_element_type=jnp.float32)
            hidden = (jax.nn.silu(gate_act) * up_act).astype(jnp.bfloat16)
            expert_out = jnp.dot(hidden, w_d, preferred_element_type=jnp.float32)
            moe_sum = moe_sum + gate_weights(idf, prf, expert)[:, None] * expert_out
            gate_b = jnp.dot(xb_now, w_g, preferred_element_type=jnp.float32)
            up_b = jnp.dot(xb_now, w_u, preferred_element_type=jnp.float32)
            silu_gate = jax.nn.silu(gate_b)
            hidden_b = (silu_gate * up_b).astype(jnp.bfloat16)
            out_b = jnp.dot(hidden_b, w_d, preferred_element_type=jnp.float32)
            inner = jnp.sum(grad_f32 * out_b, axis=-1)
            dprob_now = dprob_now + jnp.where(idb == expert, inner[:, None], 0.0)
            grad_rows = (gate_weights(idb, prb, expert)[:, None] * grad_f32).astype(jnp.bfloat16)
            grad_hidden = jnp.dot(grad_rows, w_d.T, preferred_element_type=jnp.float32)
            sig = jax.nn.sigmoid(gate_b)
            dsilu = sig * (1.0 + gate_b * (1.0 - sig))
            grad_gate = (grad_hidden * up_b * dsilu).astype(jnp.bfloat16)
            grad_up = (grad_hidden * silu_gate).astype(jnp.bfloat16)
            grad_sum = grad_sum + jnp.dot(grad_gate, w_g.T, preferred_element_type=jnp.float32)
            grad_sum = grad_sum + jnp.dot(grad_up, w_u.T, preferred_element_type=jnp.float32)
        outputs.append((x_now.astype(jnp.float32) + moe_sum).astype(jnp.bfloat16))
        grads.append((grad_f32 + grad_sum).astype(jnp.bfloat16))
        dprobs.append(dprob_now)
    fwd_next = jnp.concatenate([outputs[(segment - 1) % N_SEGMENT] for segment in range(N_SEGMENT)], axis=0)
    bwd_next = jnp.concatenate([grads[(segment + 1) % N_SEGMENT] for segment in range(N_SEGMENT)], axis=0)
    return fwd_next, bwd_next, jnp.concatenate(dprobs, axis=0)
```

```python
import jax
import jax.numpy as jnp
from jax import lax
from jax.experimental import pallas as pl
from jax.experimental.pallas import tpu as pltpu
from jax.sharding import PartitionSpec as P

EXP_WIN = 8
SIDE = 4
LANES = 128
CHUNKS = 4
STRIDE = {"z": 1, "x": 4, "y": 16}
F32 = jnp.float32
BF16 = jnp.bfloat16


def swap(value, along, by):
    length = lax.axis_size("expert")
    return lax.ppermute(
        value, "expert", [(i, i ^ (by * STRIDE[along])) for i in range(length)]
    )


def passed_along(value, axis, by):
    length = lax.axis_size(axis)
    return lax.ppermute(value, axis, [(i, (i + by) % length) for i in range(length)])


def handed_on(forth, back):
    length = lax.axis_size("segment")
    even = lax.axis_index("segment") % 2 == 0
    near = [(i, i ^ 1) for i in range(length)]
    far = [(i, (i - 1 if i % 2 == 0 else i + 1) % length) for i in range(length)]
    got_far = lax.ppermute(jnp.where(even, back, forth), "segment", far)
    got_near = lax.ppermute(jnp.where(even, forth, back), "segment", near)
    return jnp.where(even, got_far, got_near), jnp.where(even, got_near, got_far)


def gathered(value, along):
    return jnp.concatenate([value] + [swap(value, along, j) for j in range(1, SIDE)], axis=0)


def relayed(value, along):
    one, three = swap(value, along, 1), swap(value, along, 3)
    low, high = halves(three, one)
    return [value, one, swap(low, along, 1), swap(high, along, 3), three]


def scattered(own, others, along):
    for j, block in enumerate(others, 1):
        own = own + swap(block, along, j).astype(F32)
    return own


def cut(value, sent_as):
    blocks = value.reshape(SIDE, value.shape[0] // SIDE, value.shape[1])
    return blocks[0], [blocks[j].astype(sent_as) for j in range(1, SIDE)]


def to_other_order(value):
    rows, width = value.shape
    parts = value.reshape(SIDE, SIDE, rows // SIDE // SIDE, width)
    return parts.transpose(1, 0, 2, 3).reshape(rows, width)


def blocks_swapped(value):
    size = value.shape[0] // SIDE // SIDE
    return jnp.concatenate(
        [
            value[(b * SIDE + a) * size : (b * SIDE + a + 1) * size]
            for a in range(SIDE)
            for b in range(SIDE)
        ],
        axis=0,
    )


def contract_last(left, right):
    return lax.dot_general(
        left, right, (((1,), (1,)), ((), ())), preferred_element_type=F32
    )


def dot(left, right):
    return jnp.dot(left, right, preferred_element_type=F32)


def columns(pieces, first, step):
    return jnp.concatenate([ref[:, first : first + step] for ref in pieces], axis=0)


def halves_kernel(*refs):
    count = (len(refs) - 1) // 2
    sems = refs[-1]
    copies = []
    for i, (ref, out) in enumerate(zip(refs[:count], refs[count:-1])):
        half = out.shape[0]
        first = 0 if i % 2 == 0 else half
        copies.append(pltpu.make_async_copy(ref.at[pl.ds(first, half), :], out, sems.at[i]))
    for copy in copies:
        copy.start()
    for copy in copies:
        copy.wait()


def halves(*pieces):
    vmem = pl.BlockSpec(memory_space=pltpu.VMEM)
    shapes = [jax.ShapeDtypeStruct((p.shape[0] // 2, p.shape[1]), p.dtype) for p in pieces]
    return pl.pallas_call(
        halves_kernel,
        out_shape=shapes,
        in_specs=[vmem] * len(pieces),
        out_specs=[vmem] * len(pieces),
        scratch_shapes=[pltpu.SemaphoreType.DMA((len(pieces),))],
        compiler_params=pltpu.CompilerParams(vmem_limit_bytes=16 * 2**20),
    )(*pieces)


def forward_kernel(*refs):
    parts, tab_ref, hbm = refs[:5], refs[5], refs[6:9]
    wg, wu, wd, gate_b, up_b = refs[9:14]
    own, one_lo, one_hi, two_lo, two_hi, three_lo, three_hi, sems = refs[14:]
    width = wg.shape[0]
    step = width // CHUNKS
    rows = parts[0].shape[0]
    count, half = SIDE * rows, rows // 2

    def copies(c):
        part = pl.ds(c * step, step)
        return (
            pltpu.make_async_copy(hbm[0].at[part, :], wg.at[part, :], sems.at[0, c]),
            pltpu.make_async_copy(hbm[1].at[part, :], wu.at[part, :], sems.at[1, c]),
        )

    last = pltpu.make_async_copy(hbm[2], wd, sems.at[2, 0])
    for c in range(CHUNKS):
        for copy in copies(c):
            copy.start()
    last.start()
    gate = up = gate_back = up_back = 0.0
    for c in range(CHUNKS):
        for copy in copies(c):
            copy.wait()
        at = c * step
        w_g, w_u = wg[at : at + step, :], wu[at : at + step, :]
        x = columns(parts, at, step)
        gate, up = gate + dot(x, w_g), up + dot(x, w_u)
        if c * 2 < CHUNKS:
            x = columns(parts, width + at, step)
            gate_back, up_back = gate_back + dot(x, w_g), up_back + dot(x, w_u)
    gate_b[...] = blocks_swapped(gate_back)
    up_b[...] = blocks_swapped(up_back)

    hidden = (gate / (1.0 + jnp.exp(-gate)) * up).astype(BF16)
    weight = tab_ref[0][:, :1]
    last.wait()
    for c in range(CHUNKS):
        part = slice(c * step, (c + 1) * step)
        out = weight * dot(hidden, wd[:, part])
        own[:, part] = out[:rows]
        sent = out.astype(BF16)
        one_lo[:, part] = sent[rows : rows + half]
        one_hi[:, part] = out[rows + half : 2 * rows]
        two_lo[:, part] = sent[2 * rows : 2 * rows + half]
        two_hi[:, part] = sent[2 * rows + half : 3 * rows]
        three_lo[:, part] = out[3 * rows : 3 * rows + half]
        three_hi[:, part] = sent[3 * rows + half :]


def forward(parts, table, w_g, w_u, w_d):
    width, hidden = w_g.shape
    rows = parts[0].shape[0]
    half, count = rows // 2, SIDE * rows
    vmem = pl.BlockSpec(memory_space=pltpu.VMEM)
    out = jax.ShapeDtypeStruct
    return pl.pallas_call(
        forward_kernel,
        out_shape=(
            out(w_g.shape, BF16),
            out(w_u.shape, BF16),
            out(w_d.shape, BF16),
            out((count, hidden), F32),
            out((count, hidden), F32),
            out((rows, width), F32),
            out((half, width), BF16),
            out((half, width), F32),
            out((half, width), BF16),
            out((half, width), BF16),
            out((half, width), F32),
            out((half, width), BF16),
        ),
        in_specs=[vmem] * 6 + [pl.BlockSpec(memory_space=pl.ANY)] * 3,
        out_specs=(vmem,) * 12,
        scratch_shapes=[pltpu.SemaphoreType.DMA((3, CHUNKS))],
        compiler_params=pltpu.CompilerParams(vmem_limit_bytes=36 * 2**20),
        cost_estimate=pl.CostEstimate(
            flops=2 * count * width * hidden * 4, bytes_accessed=6 * width * hidden, transcendentals=0
        ),
    )(*parts, table, w_g, w_u, w_d)


def backward_kernel(*refs):
    parts, (gate_b, up_b, tab_ref, wg, wu, wd) = refs[:5], refs[5:11]
    own, one, two, three, p_own = refs[11:]
    width = wg.shape[0]
    half_width, step = width // 2, width // CHUNKS
    rows = parts[0].shape[0]
    gate, up, back = gate_b[...], up_b[...], 0.0
    for c in range(CHUNKS):
        at = c * step
        back = back + contract_last(columns(parts, at, step), wd[:, at : at + step])
        if c * 2 >= CHUNKS:
            x = columns(parts, at + half_width, step)
            gate = gate + dot(x, wg[at : at + step, :])
            up = up + dot(x, wu[at : at + step, :])

    sig = 1.0 / (1.0 + jnp.exp(-gate))
    silu = gate * sig
    hidden = (silu * up).astype(BF16)
    inner = jnp.sum(hidden.astype(F32) * back, axis=-1, keepdims=True)
    grad_hidden = tab_ref[1][:, :1] * back
    dsilu = sig * (1.0 + gate * (1.0 - sig))
    grad_gate = (grad_hidden * up * dsilu).astype(BF16)
    grad_up = (grad_hidden * silu).astype(BF16)

    prob = tab_ref[2] * inner
    p_own[...] = prob[:rows]
    top = prob.astype(BF16).astype(F32)
    lane = lax.broadcasted_iota(jnp.int32, prob.shape, 1)
    coded = jnp.where(lane < 4, top, jnp.where(lane < 8, prob - top, 0.0)).astype(BF16)
    for j, ref in enumerate((one, two, three), 1):
        ref[:, width:] = coded[j * rows : (j + 1) * rows]
    for c in range(CHUNKS):
        part = slice(c * step, (c + 1) * step)
        out = contract_last(grad_gate, wg[part, :]) + contract_last(grad_up, wu[part, :])
        own[:, part] = out[:rows]
        sent = out.astype(BF16)
        for j, ref in enumerate((one, two, three), 1):
            ref[:, part] = sent[j * rows : (j + 1) * rows]


def backward(parts, gate_b, up_b, table, w_g, w_u, w_d):
    width, hidden = w_g.shape
    rows = parts[0].shape[0]
    vmem = pl.BlockSpec(memory_space=pltpu.VMEM)
    out = jax.ShapeDtypeStruct
    sent = out((rows, width + LANES), BF16)
    return pl.pallas_call(
        backward_kernel,
        out_shape=(out((rows, width), F32), sent, sent, sent, out((rows, LANES), F32)),
        in_specs=[vmem] * 11,
        out_specs=(vmem,) * 5,
        compiler_params=pltpu.CompilerParams(vmem_limit_bytes=24 * 2**20),
    )(*parts, gate_b, up_b, table, w_g, w_u, w_d)


def own_weight(ids, probs, expert_id):
    return jnp.sum(jnp.where(ids == expert_id, probs.astype(F32), 0.0), axis=-1)


def reordered(table, order):
    hit = order[:, None] == jnp.arange(table.shape[0], dtype=jnp.int32)[None, :]
    return jnp.sum(jnp.where(hit[:, :, None], table[None, :, :], 0.0), axis=1)


def body(x_fwd, ids_fwd, probs_fwd, x_bwd, ids_bwd, probs_bwd, grad_out, w_gate, w_up, w_down):
    width = x_fwd.shape[1]
    half = width // 2
    me = lax.axis_index("expert")
    expert_id = me // (lax.axis_size("expert") // EXP_WIN)

    spot = jnp.arange(SIDE**3 * 2, dtype=jnp.int32)
    order_a = ((spot // 2) ^ me) * 2 + spot % 2
    order_b = to_other_order(order_a[:, None])[:, 0]
    weight_f = own_weight(ids_fwd, probs_fwd, expert_id)
    weight_b = own_weight(ids_bwd, probs_bwd, expert_id)
    mine_b = (ids_bwd == expert_id).astype(F32)
    tab_f = reordered(weight_f[:, None], order_a)
    tab_b = reordered(jnp.concatenate([weight_b[:, None], mine_b], axis=1), order_b)
    spread = lambda v: jnp.broadcast_to(v, (v.shape[0], LANES))
    table = jnp.stack(
        [spread(tab_f), spread(tab_b[:, :1]), jnp.tile(tab_b[:, 1:], (1, LANES // 4))]
    )

    first = jnp.concatenate([x_fwd, x_bwd[:, :half], grad_out, x_bwd[:, half:]], axis=1)
    lines = gathered(first, "z")
    a_part, b_part = lines[:, : width + half], lines[:, width + half :]
    a_parts = relayed(gathered(a_part, "x"), "y")
    b_parts = relayed(gathered(b_part, "y"), "x")

    (
        w_g, w_u, w_d, gate_b, up_b,
        f_own, f_one_lo, f_one_hi, f_two_lo, f_two_hi, f_three_lo, f_three_hi,
    ) = forward(a_parts, table, w_gate[0], w_up[0], w_down[0])
    b_own, b_one, b_two, b_three, p_own = backward(b_parts, gate_b, up_b, table, w_g, w_u, w_d)

    f_three_lo = (f_three_lo + swap(f_two_lo, "y", 1).astype(F32)).astype(BF16)
    f_one_hi = (f_one_hi + swap(f_two_hi, "y", 3).astype(F32)).astype(BF16)
    sum_f = (
        f_own
        + swap(jnp.concatenate([f_one_lo, f_one_hi], axis=0), "y", 1).astype(F32)
        + swap(jnp.concatenate([f_three_lo, f_three_hi], axis=0), "y", 3).astype(F32)
    )
    sum_b, sum_p = b_own, p_own[:, :4]
    for j, block in enumerate((b_one, b_two, b_three), 1):
        got = swap(block, "x", j).astype(F32)
        sum_b = sum_b + got[:, :width]
        sum_p = sum_p + got[:, width : width + 4] + got[:, width + 4 : width + 8]

    sum_f = scattered(*cut(sum_f, BF16), "x")
    top = lax.reduce_precision(sum_p, 8, 7)
    coded = jnp.pad(jnp.concatenate([top, sum_p - top], axis=1), ((0, 0), (0, LANES - 8)))
    both = scattered(*cut(jnp.concatenate([sum_b, coded], axis=1), BF16), "y")
    sum_b, coded = both[:, :width], both[:, width:]
    last = scattered(*cut(jnp.concatenate([sum_f, sum_b, coded], axis=1), F32), "z")

    layer_out = (x_fwd.astype(F32) + last[:, :width]).astype(BF16)
    input_grad = (grad_out.astype(F32) + last[:, width : 2 * width]).astype(BF16)
    fwd_next, bwd_next = handed_on(layer_out, input_grad)
    dprob = last[:, 2 * width : 2 * width + 4] + last[:, 2 * width + 4 : 2 * width + 8]
    return (fwd_next, bwd_next, dprob)


def solution(mesh):
    return jax.shard_map(
        body,
        mesh=mesh,
        in_specs=(
            P(("segment", "expert"), None),
            P("segment", None),
            P("segment", None),
            P(("segment", "expert"), None),
            P("segment", None),
            P("segment", None),
            P(("segment", "expert"), None),
            P("segment", None, "expert"),
            P("segment", None, "expert"),
            P("segment", "expert", None),
        ),
        out_specs=(
            P(("segment", "expert"), None),
            P(("segment", "expert"), None),
            P(("segment", "expert"), None),
        ),
        check_vma=False,
    )
```

```python
import jax
import jax.numpy as jnp
from jax import lax
from jax.experimental import pallas as pl
from jax.experimental.pallas import tpu as pltpu
from jax.sharding import PartitionSpec as P

EXP_WIN = 8
SIDE = 4
LANES = 128
CHUNKS = 2
LOAD_CHUNKS = 4
LOADS = [(kind, c) for c in range(LOAD_CHUNKS) for kind in (0, 1)]
LOADS = LOADS + [(2, c) for c in range(LOAD_CHUNKS)]
STRIDE = {"z": 1, "x": 4, "y": 16}
F32 = jnp.float32
BF16 = jnp.bfloat16


def swap(value, along, by):
    length = lax.axis_size("expert")
    return lax.ppermute(
        value, "expert", [(i, i ^ (by * STRIDE[along])) for i in range(length)]
    )


def passed_along(value, axis, by):
    length = lax.axis_size(axis)
    return lax.ppermute(value, axis, [(i, (i + by) % length) for i in range(length)])


def handed_on(forth, back):
    length = lax.axis_size("segment")
    even = lax.axis_index("segment") % 2 == 0
    near = [(i, i ^ 1) for i in range(length)]
    far = [(i, (i - 1 if i % 2 == 0 else i + 1) % length) for i in range(length)]
    got_far = lax.ppermute(jnp.where(even, back, forth), "segment", far)
    got_near = lax.ppermute(jnp.where(even, forth, back), "segment", near)
    return jnp.where(even, got_far, got_near), jnp.where(even, got_near, got_far)


def coded(value):
    top = lax.reduce_precision(value, 8, 7)
    return jnp.pad(jnp.concatenate([top, value - top], axis=1), ((0, 0), (0, LANES - 8)))


def decoded(columns_of):
    return columns_of[:, :4] + columns_of[:, 4:8]


def after(value, *earlier):
    return lax.optimization_barrier((value,) + earlier)[0]


def gathered(value, along):
    return jnp.concatenate([value] + [swap(value, along, j) for j in range(1, SIDE)], axis=0)


def relayed(value, along, earlier):
    one, three = swap(value, along, 1), swap(value, along, 3)
    low, high = halves(three, one, earlier)
    return [value, one, swap(low, along, 1), swap(high, along, 3), three]


def scattered(own, others, along):
    for j, block in enumerate(others, 1):
        own = own + swap(block, along, j).astype(F32)
    return own


def cut(value, sent_as):
    blocks = value.reshape(SIDE, value.shape[0] // SIDE, value.shape[1])
    return blocks[0], [blocks[j].astype(sent_as) for j in range(1, SIDE)]


def to_other_order(value):
    rows, width = value.shape
    parts = value.reshape(SIDE, SIDE, rows // SIDE // SIDE, width)
    return parts.transpose(1, 0, 2, 3).reshape(rows, width)


def blocks_swapped(value):
    size = value.shape[0] // SIDE // SIDE
    return jnp.concatenate(
        [
            value[(b * SIDE + a) * size : (b * SIDE + a + 1) * size]
            for a in range(SIDE)
            for b in range(SIDE)
        ],
        axis=0,
    )


def contract_last(left, right):
    return lax.dot_general(
        left, right, (((1,), (1,)), ((), ())), preferred_element_type=F32
    )


def dot(left, right):
    return jnp.dot(left, right, preferred_element_type=F32)


def columns(pieces, first, step):
    return jnp.concatenate([ref[:, first : first + step] for ref in pieces], axis=0)


def halves_kernel(three, one, _, __, low, high, sems):
    half = low.shape[0]
    copies = (
        pltpu.make_async_copy(three.at[pl.ds(0, half), :], low, sems.at[0]),
        pltpu.make_async_copy(one.at[pl.ds(half, half), :], high, sems.at[1]),
    )
    for copy in copies:
        copy.start()
    for copy in copies:
        copy.wait()


def halves(three, one, earlier):
    vmem, there = pl.BlockSpec(memory_space=pltpu.VMEM), pl.BlockSpec(memory_space=pl.ANY)
    rows, width = one.shape
    out = jax.ShapeDtypeStruct((rows // 2, width), one.dtype)
    return pl.pallas_call(
        halves_kernel,
        out_shape=(out, out),
        in_specs=[vmem, vmem, there, there],
        out_specs=(vmem, vmem),
        cost_estimate=pl.CostEstimate(flops=1, bytes_accessed=10**6, transcendentals=0),
        scratch_shapes=[pltpu.SemaphoreType.DMA((2,))],
        compiler_params=pltpu.CompilerParams(vmem_limit_bytes=16 * 2**20),
    )(three, one, *earlier)


def forward_kernel(*refs):
    parts, tab_ref, hbm = refs[:5], refs[5], refs[6:9]
    wg, wu, wd, gate_b, up_b = refs[9:14]
    own, one_lo, one_hi, two_lo, two_hi, three_lo, three_hi, sems = refs[14:]
    width = wg.shape[0]
    step = width // LOAD_CHUNKS
    rows = parts[0].shape[0]
    count, half = SIDE * rows, rows // 2

    def load(kind, c):
        part = pl.ds(c * step, step)
        at = (slice(None), part) if kind == 2 else (part, slice(None))
        held = (wg, wu, wd)[kind]
        return pltpu.make_async_copy(hbm[kind].at[at], held.at[at], sems.at[kind, c])

    for kind, c in LOADS:
        load(kind, c).start()
    gate = up = gate_back = up_back = 0.0
    for c in range(LOAD_CHUNKS):
        at = c * step
        load(0, c).wait()
        load(1, c).wait()
        w_g, w_u = wg[at : at + step, :], wu[at : at + step, :]
        x = columns(parts, at, step)
        gate, up = gate + dot(x, w_g), up + dot(x, w_u)
        if c * 2 < LOAD_CHUNKS:
            x = columns(parts, width + at, step)
            gate_back, up_back = gate_back + dot(x, w_g), up_back + dot(x, w_u)
    gate_b[...] = blocks_swapped(gate_back)
    up_b[...] = blocks_swapped(up_back)

    hidden = (gate / (1.0 + jnp.exp(-gate)) * up).astype(BF16)
    weight = tab_ref[...]
    for c in range(LOAD_CHUNKS):
        load(2, c).wait()
        part = slice(c * step, (c + 1) * step)
        out = weight * dot(hidden, wd[:, part])
        own[:, part] = out[:rows]
        sent = out.astype(BF16)
        one_lo[:, part] = sent[rows : rows + half]
        one_hi[:, part] = out[rows + half : 2 * rows]
        two_lo[:, part] = sent[2 * rows : 2 * rows + half]
        two_hi[:, part] = sent[2 * rows + half : 3 * rows]
        three_lo[:, part] = out[3 * rows : 3 * rows + half]
        three_hi[:, part] = sent[3 * rows + half :]


def forward(parts, table, w_g, w_u, w_d):
    width, hidden = w_g.shape
    rows = parts[0].shape[0]
    half, count = rows // 2, SIDE * rows
    vmem = pl.BlockSpec(memory_space=pltpu.VMEM)
    out = jax.ShapeDtypeStruct
    return pl.pallas_call(
        forward_kernel,
        out_shape=(
            out(w_g.shape, BF16),
            out(w_u.shape, BF16),
            out(w_d.shape, BF16),
            out((count, hidden), F32),
            out((count, hidden), F32),
            out((rows, width), F32),
            out((half, width), BF16),
            out((half, width), F32),
            out((half, width), BF16),
            out((half, width), BF16),
            out((half, width), F32),
            out((half, width), BF16),
        ),
        in_specs=[vmem] * 6 + [pl.BlockSpec(memory_space=pl.ANY)] * 3,
        out_specs=(vmem,) * 12,
        scratch_shapes=[pltpu.SemaphoreType.DMA((3, LOAD_CHUNKS))],
        compiler_params=pltpu.CompilerParams(vmem_limit_bytes=36 * 2**20),
        cost_estimate=pl.CostEstimate(flops=10**10, bytes_accessed=10**7, transcendentals=0),
    )(*parts, table, w_g, w_u, w_d)


def backward_kernel(*refs):
    parts, (gate_b, up_b, tab_ref, wg, wu, wd) = refs[:5], refs[5:11]
    own, one, two, three, p_own = refs[11:]
    width = wg.shape[0]
    half_width, step = width // 2, width // CHUNKS
    rows = parts[0].shape[0]
    gate, up, back = gate_b[...], up_b[...], 0.0
    for c in range(CHUNKS):
        at = c * step
        back = back + contract_last(columns(parts, at, step), wd[:, at : at + step])
        if c * 2 >= CHUNKS:
            x = columns(parts, at + half_width, step)
            gate = gate + dot(x, wg[at : at + step, :])
            up = up + dot(x, wu[at : at + step, :])

    sig = 1.0 / (1.0 + jnp.exp(-gate))
    silu = gate * sig
    hidden = (silu * up).astype(BF16)
    inner = jnp.sum(hidden.astype(F32) * back, axis=-1, keepdims=True)
    grad_hidden = tab_ref[:, 8:9] * back
    dsilu = sig * (1.0 + gate * (1.0 - sig))
    grad_gate = (grad_hidden * up * dsilu).astype(BF16)
    grad_up = (grad_hidden * silu).astype(BF16)

    prob = tab_ref[:, :8] * inner
    p_own[...] = prob[:rows]
    top = prob.astype(BF16).astype(F32)
    lane = lax.broadcasted_iota(jnp.int32, prob.shape, 1)
    parts_of = jnp.where(lane < 4, top, prob - top).astype(BF16)
    for j, ref in enumerate((one, two, three), 1):
        ref[:, width:] = jnp.zeros((rows, LANES), BF16)
        ref[:, width : width + 8] = parts_of[j * rows : (j + 1) * rows]
    for c in range(CHUNKS):
        part = slice(c * step, (c + 1) * step)
        out = contract_last(grad_gate, wg[part, :]) + contract_last(grad_up, wu[part, :])
        own[:, part] = out[:rows]
        sent = out.astype(BF16)
        for j, ref in enumerate((one, two, three), 1):
            ref[:, part] = sent[j * rows : (j + 1) * rows]


def backward(parts, gate_b, up_b, table, w_g, w_u, w_d):
    width, hidden = w_g.shape
    rows = parts[0].shape[0]
    vmem = pl.BlockSpec(memory_space=pltpu.VMEM)
    out = jax.ShapeDtypeStruct
    sent = out((rows, width + LANES), BF16)
    return pl.pallas_call(
        backward_kernel,
        out_shape=(out((rows, width), F32), sent, sent, sent, out((rows, 8), F32)),
        in_specs=[vmem] * 11,
        out_specs=(vmem,) * 5,
        cost_estimate=pl.CostEstimate(flops=10**10, bytes_accessed=10**7, transcendentals=0),
        compiler_params=pltpu.CompilerParams(vmem_limit_bytes=24 * 2**20),
    )(*parts, gate_b, up_b, table, w_g, w_u, w_d)


def own_weight(ids, probs, expert_id):
    return jnp.sum(jnp.where(ids == expert_id, probs.astype(F32), 0.0), axis=-1)


def reordered(table, order):
    hit = order[:, None] == jnp.arange(table.shape[0], dtype=jnp.int32)[None, :]
    return jnp.sum(jnp.where(hit[:, :, None], table[None, :, :], 0.0), axis=1)


def body(x_fwd, ids_fwd, probs_fwd, x_bwd, ids_bwd, probs_bwd, grad_out, w_gate, w_up, w_down):
    width = x_fwd.shape[1]
    half = width // 2
    me = lax.axis_index("expert")
    expert_id = me // (lax.axis_size("expert") // EXP_WIN)

    spot = jnp.arange(SIDE**3 * 2, dtype=jnp.int32)
    order_a = ((spot // 2) ^ me) * 2 + spot % 2
    order_b = to_other_order(order_a[:, None])[:, 0]
    weight_f = own_weight(ids_fwd, probs_fwd, expert_id)
    weight_b = own_weight(ids_bwd, probs_bwd, expert_id)
    mine_b = (ids_bwd == expert_id).astype(F32)
    tab_f = reordered(weight_f[:, None], order_a)
    tab_b = reordered(jnp.concatenate([mine_b, mine_b, weight_b[:, None]], axis=1), order_b)
    tables = tab_f, tab_b

    first = jnp.concatenate([x_fwd, x_bwd[:, :half], grad_out, x_bwd[:, half:]], axis=1)
    lines = gathered(first, "z")
    a_part, b_part = lines[:, : width + half], lines[:, width + half :]
    a_parts = relayed(gathered(a_part, "x"), "y", tables)
    b_parts = relayed(gathered(b_part, "y"), "x", tables)

    (
        w_g, w_u, w_d, gate_b, up_b,
        f_own, f_one_lo, f_one_hi, f_two_lo, f_two_hi, f_three_lo, f_three_hi,
    ) = forward(a_parts, tab_f, w_gate[0], w_up[0], w_down[0])
    b_own, b_one, b_two, b_three, p_own = backward(b_parts, gate_b, up_b, tab_b, w_g, w_u, w_d)

    f_two_lo, f_two_hi = after(f_two_lo, b_own), after(f_two_hi, b_own)

    f_three_lo = (f_three_lo + swap(f_two_lo, "y", 1).astype(F32)).astype(BF16)
    f_one_hi = (f_one_hi + swap(f_two_hi, "y", 3).astype(F32)).astype(BF16)
    sum_f = (
        f_own
        + swap(jnp.concatenate([f_one_lo, f_one_hi], axis=0), "y", 1).astype(F32)
        + swap(jnp.concatenate([f_three_lo, f_three_hi], axis=0), "y", 3).astype(F32)
    )
    sum_b, sum_p = after(b_own, sum_f), p_own[:, :4]
    for j, block in enumerate((b_one, b_two, b_three), 1):
        got = swap(block, "x", j).astype(F32)
        sum_b = sum_b + got[:, :width]
        sum_p = sum_p + got[:, width : width + 4] + got[:, width + 4 : width + 8]

    sum_f = scattered(*cut(sum_f, BF16), "x")
    both = scattered(*cut(jnp.concatenate([sum_b, coded(sum_p)], axis=1), BF16), "y")
    sum_b, sum_p = both[:, :width], decoded(both[:, width:])
    last = scattered(*cut(jnp.concatenate([sum_f, sum_b, coded(sum_p)], axis=1), F32), "z")

    layer_out = (x_fwd.astype(F32) + last[:, :width]).astype(BF16)
    input_grad = (grad_out.astype(F32) + last[:, width : 2 * width]).astype(BF16)
    fwd_next, bwd_next = handed_on(layer_out, input_grad)
    dprob = last[:, 2 * width : 2 * width + 4] + last[:, 2 * width + 4 : 2 * width + 8]
    return (fwd_next, bwd_next, dprob)


def solution(mesh):
    return jax.shard_map(
        body,
        mesh=mesh,
        in_specs=(
            P(("segment", "expert"), None),
            P("segment", None),
            P("segment", None),
            P(("segment", "expert"), None),
            P("segment", None),
            P("segment", None),
            P(("segment", "expert"), None),
            P("segment", None, "expert"),
            P("segment", None, "expert"),
            P("segment", "expert", None),
        ),
        out_specs=(
            P(("segment", "expert"), None),
            P(("segment", "expert"), None),
            P(("segment", "expert"), None),
        ),
        check_vma=False,
    )
```

```python
import jax
import jax.numpy as jnp
from jax import lax
from jax.experimental import pallas as pl
from jax.experimental.pallas import tpu as pltpu
from jax.sharding import PartitionSpec as P

EXP_WIN = 8
SIDE = 4
LANES = 128
CHUNKS = 2
LOAD_CHUNKS = 4
LOADS = [(kind, c) for c in range(LOAD_CHUNKS) for kind in (0, 1)]
LOADS = LOADS + [(2, c) for c in range(LOAD_CHUNKS)]
STRIDE = {"z": 1, "x": 4, "y": 16}
F32 = jnp.float32
BF16 = jnp.bfloat16


def swap(value, along, by):
    length = lax.axis_size("expert")
    return lax.ppermute(
        value, "expert", [(i, i ^ (by * STRIDE[along])) for i in range(length)]
    )


def passed_along(value, axis, by):
    length = lax.axis_size(axis)
    return lax.ppermute(value, axis, [(i, (i + by) % length) for i in range(length)])


def handed_on(forth, back):
    length = lax.axis_size("segment")
    even = lax.axis_index("segment") % 2 == 0
    near = [(i, i ^ 1) for i in range(length)]
    far = [(i, (i - 1 if i % 2 == 0 else i + 1) % length) for i in range(length)]
    got_far = lax.ppermute(jnp.where(even, back, forth), "segment", far)
    got_near = lax.ppermute(jnp.where(even, forth, back), "segment", near)
    return jnp.where(even, got_far, got_near), jnp.where(even, got_near, got_far)


def coded(value):
    top = lax.reduce_precision(value, 8, 7)
    return jnp.pad(jnp.concatenate([top, value - top], axis=1), ((0, 0), (0, LANES - 8)))


def decoded(columns_of):
    return columns_of[:, :4] + columns_of[:, 4:8]


def after(value, *earlier):
    return lax.optimization_barrier((value,) + earlier)[0]


def gathered(value, along):
    return jnp.concatenate([value] + [swap(value, along, j) for j in range(1, SIDE)], axis=0)


def relayed(value, along, earlier):
    one, three = swap(value, along, 1), swap(value, along, 3)
    low, high = halves(three, one, earlier)
    return [value, one, swap(low, along, 1), swap(high, along, 3), three]


def scattered(own, others, along):
    for j, block in enumerate(others, 1):
        own = own + swap(block, along, j).astype(F32)
    return own


def cut(value, sent_as):
    blocks = value.reshape(SIDE, value.shape[0] // SIDE, value.shape[1])
    return blocks[0], [blocks[j].astype(sent_as) for j in range(1, SIDE)]


def to_other_order(value):
    rows, width = value.shape
    parts = value.reshape(SIDE, SIDE, rows // SIDE // SIDE, width)
    return parts.transpose(1, 0, 2, 3).reshape(rows, width)


def blocks_swapped(value):
    size = value.shape[0] // SIDE // SIDE
    return jnp.concatenate(
        [
            value[(b * SIDE + a) * size : (b * SIDE + a + 1) * size]
            for a in range(SIDE)
            for b in range(SIDE)
        ],
        axis=0,
    )


def contract_last(left, right):
    return lax.dot_general(
        left, right, (((1,), (1,)), ((), ())), preferred_element_type=F32
    )


def dot(left, right):
    return jnp.dot(left, right, preferred_element_type=F32)


def columns(pieces, first, step):
    return jnp.concatenate([ref[:, first : first + step] for ref in pieces], axis=0)


def halves_kernel(three, one, _, __, low, high, sems):
    half = low.shape[0]
    copies = (
        pltpu.make_async_copy(three.at[pl.ds(0, half), :], low, sems.at[0]),
        pltpu.make_async_copy(one.at[pl.ds(half, half), :], high, sems.at[1]),
    )
    for copy in copies:
        copy.start()
    for copy in copies:
        copy.wait()


def halves(three, one, earlier):
    vmem, there = pl.BlockSpec(memory_space=pltpu.VMEM), pl.BlockSpec(memory_space=pl.ANY)
    rows, width = one.shape
    out = jax.ShapeDtypeStruct((rows // 2, width), one.dtype)
    return pl.pallas_call(
        halves_kernel,
        out_shape=(out, out),
        in_specs=[vmem, vmem, there, there],
        out_specs=(vmem, vmem),
        cost_estimate=pl.CostEstimate(flops=1, bytes_accessed=10**6, transcendentals=0),
        scratch_shapes=[pltpu.SemaphoreType.DMA((2,))],
        compiler_params=pltpu.CompilerParams(vmem_limit_bytes=16 * 2**20),
    )(three, one, *earlier)


def forward_kernel(*refs):
    parts, tab_ref, hbm = refs[:5], refs[5], refs[6:9]
    wg, wu, wd, gate_b, up_b = refs[9:14]
    own, one, two, three, sems = refs[14:]
    width = wg.shape[0]
    step = width // LOAD_CHUNKS
    rows = parts[0].shape[0]

    def load(kind, c):
        part = pl.ds(c * step, step)
        at = (slice(None), part) if kind == 2 else (part, slice(None))
        held = (wg, wu, wd)[kind]
        return pltpu.make_async_copy(hbm[kind].at[at], held.at[at], sems.at[kind, c])

    for kind, c in LOADS:
        load(kind, c).start()
    gate = up = gate_back = up_back = 0.0
    for c in range(LOAD_CHUNKS):
        at = c * step
        load(0, c).wait()
        load(1, c).wait()
        w_g, w_u = wg[at : at + step, :], wu[at : at + step, :]
        x = columns(parts, at, step)
        gate, up = gate + dot(x, w_g), up + dot(x, w_u)
        if c * 2 < LOAD_CHUNKS:
            x = columns(parts, width + at, step)
            gate_back, up_back = gate_back + dot(x, w_g), up_back + dot(x, w_u)
    gate_b[...] = blocks_swapped(gate_back)
    up_b[...] = blocks_swapped(up_back)

    hidden = (gate / (1.0 + jnp.exp(-gate)) * up).astype(BF16)
    weight = tab_ref[...]
    for c in range(LOAD_CHUNKS):
        load(2, c).wait()
        part = slice(c * step, (c + 1) * step)
        out = weight * dot(hidden, wd[:, part])
        own[:, part] = out[:rows]
        sent = out.astype(BF16)
        for j, ref in enumerate((one, two, three), 1):
            ref[:, part] = sent[j * rows : (j + 1) * rows]


def forward(parts, table, w_g, w_u, w_d):
    width, hidden = w_g.shape
    rows = parts[0].shape[0]
    count = SIDE * rows
    vmem = pl.BlockSpec(memory_space=pltpu.VMEM)
    out = jax.ShapeDtypeStruct
    return pl.pallas_call(
        forward_kernel,
        out_shape=(
            out(w_g.shape, BF16),
            out(w_u.shape, BF16),
            out(w_d.shape, BF16),
            out((count, hidden), F32),
            out((count, hidden), F32),
            out((rows, width), F32),
            out((rows, width), BF16),
            out((rows, width), BF16),
            out((rows, width), BF16),
        ),
        in_specs=[vmem] * 6 + [pl.BlockSpec(memory_space=pl.ANY)] * 3,
        out_specs=(vmem,) * 9,
        scratch_shapes=[pltpu.SemaphoreType.DMA((3, LOAD_CHUNKS))],
        compiler_params=pltpu.CompilerParams(vmem_limit_bytes=36 * 2**20),
        cost_estimate=pl.CostEstimate(flops=10**10, bytes_accessed=10**7, transcendentals=0),
    )(*parts, table, w_g, w_u, w_d)


def backward_kernel(*refs):
    parts, (gate_b, up_b, tab_ref, wg, wu, wd) = refs[:5], refs[5:11]
    own, one_lo, one_hi, two_lo, two_hi, three_lo, three_hi, p_own = refs[11:]
    blocks = (one_lo, one_hi, two_lo, two_hi, three_lo, three_hi)
    width = wg.shape[0]
    half_width, step = width // 2, width // CHUNKS
    rows = parts[0].shape[0]
    gate, up, back = gate_b[...], up_b[...], 0.0
    for c in range(CHUNKS):
        at = c * step
        back = back + contract_last(columns(parts, at, step), wd[:, at : at + step])
        if c * 2 >= CHUNKS:
            x = columns(parts, at + half_width, step)
            gate = gate + dot(x, wg[at : at + step, :])
            up = up + dot(x, wu[at : at + step, :])

    sig = 1.0 / (1.0 + jnp.exp(-gate))
    silu = gate * sig
    hidden = (silu * up).astype(BF16)
    inner = jnp.sum(hidden.astype(F32) * back, axis=-1, keepdims=True)
    grad_hidden = tab_ref[:, 8:9] * back
    dsilu = sig * (1.0 + gate * (1.0 - sig))
    grad_gate = (grad_hidden * up * dsilu).astype(BF16)
    grad_up = (grad_hidden * silu).astype(BF16)

    prob = tab_ref[:, :8] * inner
    p_own[...] = prob[:rows]
    top = prob.astype(BF16).astype(F32)
    lane = lax.broadcasted_iota(jnp.int32, prob.shape, 1)
    parts_of = jnp.where(lane < 4, top, prob - top).astype(BF16)
    half = rows // 2
    for i, ref in enumerate(blocks, 2):
        ref[:, width:] = jnp.zeros((half, LANES), ref.dtype)
        ref[:, width : width + 8] = parts_of[i * half : (i + 1) * half].astype(ref.dtype)
    for c in range(CHUNKS):
        part = slice(c * step, (c + 1) * step)
        out = contract_last(grad_gate, wg[part, :]) + contract_last(grad_up, wu[part, :])
        own[:, part] = out[:rows]
        for i, ref in enumerate(blocks, 2):
            ref[:, part] = out[i * half : (i + 1) * half].astype(ref.dtype)


def backward(parts, gate_b, up_b, table, w_g, w_u, w_d):
    width, hidden = w_g.shape
    rows = parts[0].shape[0]
    vmem = pl.BlockSpec(memory_space=pltpu.VMEM)
    out = jax.ShapeDtypeStruct
    sent = out((rows // 2, width + LANES), BF16)
    added = out((rows // 2, width + LANES), F32)
    return pl.pallas_call(
        backward_kernel,
        out_shape=(
            out((rows, width), F32), sent, added, sent, sent, added, sent, out((rows, 8), F32)
        ),
        in_specs=[vmem] * 11,
        out_specs=(vmem,) * 8,
        cost_estimate=pl.CostEstimate(flops=10**10, bytes_accessed=10**7, transcendentals=0),
        compiler_params=pltpu.CompilerParams(vmem_limit_bytes=24 * 2**20),
    )(*parts, gate_b, up_b, table, w_g, w_u, w_d)


def own_weight(ids, probs, expert_id):
    return jnp.sum(jnp.where(ids == expert_id, probs.astype(F32), 0.0), axis=-1)


def reordered(table, order):
    hit = order[:, None] == jnp.arange(table.shape[0], dtype=jnp.int32)[None, :]
    return jnp.sum(jnp.where(hit[:, :, None], table[None, :, :], 0.0), axis=1)


def body(x_fwd, ids_fwd, probs_fwd, x_bwd, ids_bwd, probs_bwd, grad_out, w_gate, w_up, w_down):
    width = x_fwd.shape[1]
    half = width // 2
    me = lax.axis_index("expert")
    expert_id = me // (lax.axis_size("expert") // EXP_WIN)

    spot = jnp.arange(SIDE**3 * 2, dtype=jnp.int32)
    order_a = ((spot // 2) ^ me) * 2 + spot % 2
    order_b = to_other_order(order_a[:, None])[:, 0]
    weight_f = own_weight(ids_fwd, probs_fwd, expert_id)
    weight_b = own_weight(ids_bwd, probs_bwd, expert_id)
    mine_b = (ids_bwd == expert_id).astype(F32)
    tab_f = reordered(weight_f[:, None], order_a)
    tab_b = reordered(jnp.concatenate([mine_b, mine_b, weight_b[:, None]], axis=1), order_b)
    tables = tab_f, tab_b

    first = jnp.concatenate([x_fwd, x_bwd[:, :half], grad_out, x_bwd[:, half:]], axis=1)
    lines = gathered(first, "z")
    a_part, b_part = lines[:, : width + half], lines[:, width + half :]
    a_parts = relayed(gathered(a_part, "x"), "y", tables)
    b_parts = relayed(gathered(b_part, "y"), "x", tables)

    w_g, w_u, w_d, gate_b, up_b, f_own, f_one, f_two, f_three = forward(
        a_parts, tab_f, w_gate[0], w_up[0], w_down[0]
    )
    b_own, b_one_lo, b_one_hi, b_two_lo, b_two_hi, b_three_lo, b_three_hi, p_own = backward(
        b_parts, gate_b, up_b, tab_b, w_g, w_u, w_d
    )

    sum_f = scattered(f_own, (f_one, f_two, f_three), "y")
    def merged(one, two):
        rest = coded(decoded(one[:, width:]) + decoded(two[:, width:].astype(F32)))
        body_of = one[:, :width] + two[:, :width].astype(F32)
        return jnp.concatenate([body_of.astype(BF16), rest.astype(BF16)], axis=1)

    b_three_lo = merged(b_three_lo, swap(b_two_lo, "x", 1))
    b_one_hi = merged(b_one_hi, swap(b_two_hi, "x", 3))
    got_one = swap(jnp.concatenate([b_one_lo, b_one_hi], axis=0), "x", 1).astype(F32)
    got_three = swap(jnp.concatenate([b_three_lo, b_three_hi], axis=0), "x", 3).astype(F32)
    sum_b = b_own + got_one[:, :width] + got_three[:, :width]
    sum_p = p_own[:, :4] + decoded(got_one[:, width:]) + decoded(got_three[:, width:])

    sum_f = scattered(*cut(sum_f, BF16), "x")
    both = scattered(*cut(jnp.concatenate([sum_b, coded(sum_p)], axis=1), BF16), "y")
    sum_b, sum_p = both[:, :width], decoded(both[:, width:])
    last = scattered(*cut(jnp.concatenate([sum_f, sum_b, coded(sum_p)], axis=1), F32), "z")

    layer_out = (x_fwd.astype(F32) + last[:, :width]).astype(BF16)
    input_grad = (grad_out.astype(F32) + last[:, width : 2 * width]).astype(BF16)
    fwd_next, bwd_next = handed_on(layer_out, input_grad)
    dprob = last[:, 2 * width : 2 * width + 4] + last[:, 2 * width + 4 : 2 * width + 8]
    return (fwd_next, bwd_next, dprob)


def solution(mesh):
    return jax.shard_map(
        body,
        mesh=mesh,
        in_specs=(
            P(("segment", "expert"), None),
            P("segment", None),
            P("segment", None),
            P(("segment", "expert"), None),
            P("segment", None),
            P("segment", None),
            P(("segment", "expert"), None),
            P("segment", None, "expert"),
            P("segment", None, "expert"),
            P("segment", "expert", None),
        ),
        out_specs=(
            P(("segment", "expert"), None),
            P(("segment", "expert"), None),
            P(("segment", "expert"), None),
        ),
        check_vma=False,
    )
```

```python
import jax
import jax.numpy as jnp
from jax import lax
from jax.experimental import pallas as pl
from jax.experimental.pallas import tpu as pltpu
from jax.sharding import PartitionSpec as P

EXP_WIN = 8
SIDE = 4
LANES = 128
CHUNKS = 2
LOAD_CHUNKS = 4
LOADS = [(kind, c) for c in range(LOAD_CHUNKS) for kind in (0, 1)]
LOADS = LOADS + [(2, c) for c in range(LOAD_CHUNKS)]
STRIDE = {"z": 1, "x": 4, "y": 16}
F32 = jnp.float32
BF16 = jnp.bfloat16


def swap(value, along, by):
    length = lax.axis_size("expert")
    return lax.ppermute(
        value, "expert", [(i, i ^ (by * STRIDE[along])) for i in range(length)]
    )


def passed_along(value, axis, by):
    length = lax.axis_size(axis)
    return lax.ppermute(value, axis, [(i, (i + by) % length) for i in range(length)])


def handed_on(forth, back):
    length = lax.axis_size("segment")
    even = lax.axis_index("segment") % 2 == 0
    near = [(i, i ^ 1) for i in range(length)]
    far = [(i, (i - 1 if i % 2 == 0 else i + 1) % length) for i in range(length)]
    got_far = lax.ppermute(jnp.where(even, back, forth), "segment", far)
    got_near = lax.ppermute(jnp.where(even, forth, back), "segment", near)
    return jnp.where(even, got_far, got_near), jnp.where(even, got_near, got_far)


def coded(value):
    top = lax.reduce_precision(value, 8, 7)
    return jnp.pad(jnp.concatenate([top, value - top], axis=1), ((0, 0), (0, LANES - 8)))


def decoded(columns_of):
    return columns_of[:, :4] + columns_of[:, 4:8]


def after(value, *earlier):
    return lax.optimization_barrier((value,) + earlier)[0]


def gathered(value, along):
    return jnp.concatenate([value] + [swap(value, along, j) for j in range(1, SIDE)], axis=0)


def relayed(value, along, earlier):
    one, three = swap(value, along, 1), swap(value, along, 3)
    low, high = halves(three, one, earlier)
    return [value, one, swap(low, along, 1), swap(high, along, 3), three]


def scattered(own, others, along):
    for j, block in enumerate(others, 1):
        own = own + swap(block, along, j).astype(F32)
    return own


def cut(value, sent_as):
    blocks = value.reshape(SIDE, value.shape[0] // SIDE, value.shape[1])
    return blocks[0], [blocks[j].astype(sent_as) for j in range(1, SIDE)]


def to_other_order(value):
    rows, width = value.shape
    parts = value.reshape(SIDE, SIDE, rows // SIDE // SIDE, width)
    return parts.transpose(1, 0, 2, 3).reshape(rows, width)


def blocks_swapped(value):
    size = value.shape[0] // SIDE // SIDE
    return jnp.concatenate(
        [
            value[(b * SIDE + a) * size : (b * SIDE + a + 1) * size]
            for a in range(SIDE)
            for b in range(SIDE)
        ],
        axis=0,
    )


def contract_last(left, right):
    return lax.dot_general(
        left, right, (((1,), (1,)), ((), ())), preferred_element_type=F32
    )


def dot(left, right):
    return jnp.dot(left, right, preferred_element_type=F32)


def columns(pieces, first, step):
    return jnp.concatenate([ref[:, first : first + step] for ref in pieces], axis=0)


def halves_kernel(three, one, _, __, low, high, sems):
    half = low.shape[0]
    copies = (
        pltpu.make_async_copy(three.at[pl.ds(0, half), :], low, sems.at[0]),
        pltpu.make_async_copy(one.at[pl.ds(half, half), :], high, sems.at[1]),
    )
    for copy in copies:
        copy.start()
    for copy in copies:
        copy.wait()


def halves(three, one, earlier):
    vmem, there = pl.BlockSpec(memory_space=pltpu.VMEM), pl.BlockSpec(memory_space=pl.ANY)
    rows, width = one.shape
    out = jax.ShapeDtypeStruct((rows // 2, width), one.dtype)
    return pl.pallas_call(
        halves_kernel,
        out_shape=(out, out),
        in_specs=[vmem, vmem, there, there],
        out_specs=(vmem, vmem),
        cost_estimate=pl.CostEstimate(flops=1, bytes_accessed=10**6, transcendentals=0),
        scratch_shapes=[pltpu.SemaphoreType.DMA((2,))],
        compiler_params=pltpu.CompilerParams(vmem_limit_bytes=16 * 2**20),
    )(three, one, *earlier)


def forward_kernel(*refs):
    parts, tab_ref, hbm = refs[:5], refs[5], refs[6:9]
    wg, wu, wd, gate_b, up_b = refs[9:14]
    own, one_lo, one_hi, two_lo, two_hi, three_lo, three_hi, sems = refs[14:]
    width = wg.shape[0]
    step = width // LOAD_CHUNKS
    rows = parts[0].shape[0]
    count, half = SIDE * rows, rows // 2

    def load(kind, c):
        part = pl.ds(c * step, step)
        at = (slice(None), part) if kind == 2 else (part, slice(None))
        held = (wg, wu, wd)[kind]
        return pltpu.make_async_copy(hbm[kind].at[at], held.at[at], sems.at[kind, c])

    for kind, c in LOADS:
        load(kind, c).start()
    gate = up = gate_back = up_back = 0.0
    for c in range(LOAD_CHUNKS):
        at = c * step
        load(0, c).wait()
        load(1, c).wait()
        w_g, w_u = wg[at : at + step, :], wu[at : at + step, :]
        x = columns(parts, at, step)
        gate, up = gate + dot(x, w_g), up + dot(x, w_u)
        if c * 2 < LOAD_CHUNKS:
            x = columns(parts, width + at, step)
            gate_back, up_back = gate_back + dot(x, w_g), up_back + dot(x, w_u)
    gate_b[...] = blocks_swapped(gate_back)
    up_b[...] = blocks_swapped(up_back)

    hidden = (gate / (1.0 + jnp.exp(-gate)) * up).astype(BF16)
    weight = tab_ref[...]
    for c in range(LOAD_CHUNKS):
        load(2, c).wait()
        part = slice(c * step, (c + 1) * step)
        out = weight * dot(hidden, wd[:, part])
        own[:, part] = out[:rows]
        sent = out.astype(BF16)
        one_lo[:, part] = sent[rows : rows + half]
        one_hi[:, part] = out[rows + half : 2 * rows]
        two_lo[:, part] = sent[2 * rows : 2 * rows + half]
        two_hi[:, part] = sent[2 * rows + half : 3 * rows]
        three_lo[:, part] = out[3 * rows : 3 * rows + half]
        three_hi[:, part] = sent[3 * rows + half :]


def forward(parts, table, w_g, w_u, w_d):
    width, hidden = w_g.shape
    rows = parts[0].shape[0]
    half, count = rows // 2, SIDE * rows
    vmem = pl.BlockSpec(memory_space=pltpu.VMEM)
    out = jax.ShapeDtypeStruct
    return pl.pallas_call(
        forward_kernel,
        out_shape=(
            out(w_g.shape, BF16),
            out(w_u.shape, BF16),
            out(w_d.shape, BF16),
            out((count, hidden), F32),
            out((count, hidden), F32),
            out((rows, width), F32),
            out((half, width), BF16),
            out((half, width), F32),
            out((half, width), BF16),
            out((half, width), BF16),
            out((half, width), F32),
            out((half, width), BF16),
        ),
        in_specs=[vmem] * 6 + [pl.BlockSpec(memory_space=pl.ANY)] * 3,
        out_specs=(vmem,) * 12,
        scratch_shapes=[pltpu.SemaphoreType.DMA((3, LOAD_CHUNKS))],
        compiler_params=pltpu.CompilerParams(vmem_limit_bytes=36 * 2**20),
        cost_estimate=pl.CostEstimate(flops=10**10, bytes_accessed=10**7, transcendentals=0),
    )(*parts, table, w_g, w_u, w_d)


def backward_kernel(*refs):
    parts, (gate_b, up_b, tab_ref, wg, wu, wd) = refs[:5], refs[5:11]
    own, one, two, three, p_own = refs[11:]
    width = wg.shape[0]
    half_width, step = width // 2, width // CHUNKS
    rows = parts[0].shape[0]
    gate, up, back = gate_b[...], up_b[...], 0.0
    for c in range(CHUNKS):
        at = c * step
        back = back + contract_last(columns(parts, at, step), wd[:, at : at + step])
        if c * 2 >= CHUNKS:
            x = columns(parts, at + half_width, step)
            gate = gate + dot(x, wg[at : at + step, :])
            up = up + dot(x, wu[at : at + step, :])

    sig = 1.0 / (1.0 + jnp.exp(-gate))
    silu = gate * sig
    hidden = (silu * up).astype(BF16)
    inner = jnp.sum(hidden.astype(F32) * back, axis=-1, keepdims=True)
    grad_hidden = tab_ref[:, 8:9] * back
    dsilu = sig * (1.0 + gate * (1.0 - sig))
    grad_gate = (grad_hidden * up * dsilu).astype(BF16)
    grad_up = (grad_hidden * silu).astype(BF16)

    prob = tab_ref[:, :8] * inner
    p_own[...] = prob[:rows]
    top = prob.astype(BF16).astype(F32)
    lane = lax.broadcasted_iota(jnp.int32, prob.shape, 1)
    parts_of = jnp.where(lane < 4, top, prob - top).astype(BF16)
    for j, ref in enumerate((one, two, three), 1):
        ref[:, width:] = jnp.zeros((rows, LANES), BF16)
        ref[:, width : width + 8] = parts_of[j * rows : (j + 1) * rows]
    for c in range(CHUNKS):
        part = slice(c * step, (c + 1) * step)
        out = contract_last(grad_gate, wg[part, :]) + contract_last(grad_up, wu[part, :])
        own[:, part] = out[:rows]
        sent = out.astype(BF16)
        for j, ref in enumerate((one, two, three), 1):
            ref[:, part] = sent[j * rows : (j + 1) * rows]


def backward(parts, gate_b, up_b, table, w_g, w_u, w_d):
    width, hidden = w_g.shape
    rows = parts[0].shape[0]
    vmem = pl.BlockSpec(memory_space=pltpu.VMEM)
    out = jax.ShapeDtypeStruct
    sent = out((rows, width + LANES), BF16)
    return pl.pallas_call(
        backward_kernel,
        out_shape=(out((rows, width), F32), sent, sent, sent, out((rows, 8), F32)),
        in_specs=[vmem] * 11,
        out_specs=(vmem,) * 5,
        cost_estimate=pl.CostEstimate(flops=10**10, bytes_accessed=10**7, transcendentals=0),
        compiler_params=pltpu.CompilerParams(vmem_limit_bytes=24 * 2**20),
    )(*parts, gate_b, up_b, table, w_g, w_u, w_d)


def own_weight(ids, probs, expert_id):
    return jnp.sum(jnp.where(ids == expert_id, probs.astype(F32), 0.0), axis=-1)


def reordered(table, order):
    hit = order[:, None] == jnp.arange(table.shape[0], dtype=jnp.int32)[None, :]
    return jnp.sum(jnp.where(hit[:, :, None], table[None, :, :], 0.0), axis=1)


def body(x_fwd, ids_fwd, probs_fwd, x_bwd, ids_bwd, probs_bwd, grad_out, w_gate, w_up, w_down):
    width = x_fwd.shape[1]
    half = width // 2
    me = lax.axis_index("expert")
    expert_id = me // (lax.axis_size("expert") // EXP_WIN)

    spot = jnp.arange(SIDE**3 * 2, dtype=jnp.int32)
    order_a = ((spot // 2) ^ me) * 2 + spot % 2
    order_b = to_other_order(order_a[:, None])[:, 0]
    weight_f = own_weight(ids_fwd, probs_fwd, expert_id)
    weight_b = own_weight(ids_bwd, probs_bwd, expert_id)
    mine_b = (ids_bwd == expert_id).astype(F32)
    tab_f = reordered(weight_f[:, None], order_a)
    tab_b = reordered(jnp.concatenate([mine_b, mine_b, weight_b[:, None]], axis=1), order_b)
    tables = tab_f, tab_b

    first = jnp.concatenate([x_fwd, x_bwd[:, :half], grad_out, x_bwd[:, half:]], axis=1)
    lines = gathered(first, "z")
    a_part, b_part = lines[:, : width + half], lines[:, width + half :]
    a_parts = relayed(gathered(a_part, "x"), "y", tables)
    b_parts = relayed(gathered(b_part, "y"), "x", tables)

    (
        w_g, w_u, w_d, gate_b, up_b,
        f_own, f_one_lo, f_one_hi, f_two_lo, f_two_hi, f_three_lo, f_three_hi,
    ) = forward(a_parts, tab_f, w_gate[0], w_up[0], w_down[0])
    b_own, b_one, b_two, b_three, p_own = backward(b_parts, gate_b, up_b, tab_b, w_g, w_u, w_d)

    f_three_lo = (f_three_lo + swap(f_two_lo, "y", 1).astype(F32)).astype(BF16)
    f_one_hi = (f_one_hi + swap(f_two_hi, "y", 3).astype(F32)).astype(BF16)
    sum_f = (
        f_own
        + swap(jnp.concatenate([f_one_lo, f_one_hi], axis=0), "y", 1).astype(F32)
        + swap(jnp.concatenate([f_three_lo, f_three_hi], axis=0), "y", 3).astype(F32)
    )
    sum_b, sum_p = after(b_own, sum_f), p_own[:, :4]
    for j, block in enumerate((b_one, b_two, b_three), 1):
        got = swap(block, "x", j).astype(F32)
        sum_b = sum_b + got[:, :width]
        sum_p = sum_p + got[:, width : width + 4] + got[:, width + 4 : width + 8]

    sum_f = scattered(*cut(sum_f, BF16), "x")
    both = scattered(*cut(jnp.concatenate([sum_b, coded(sum_p)], axis=1), BF16), "y")
    sum_b, sum_p = both[:, :width], decoded(both[:, width:])
    last = scattered(*cut(jnp.concatenate([sum_f, sum_b, coded(sum_p)], axis=1), BF16), "z")

    layer_out = (x_fwd.astype(F32) + last[:, :width]).astype(BF16)
    input_grad = (grad_out.astype(F32) + last[:, width : 2 * width]).astype(BF16)
    fwd_next, bwd_next = handed_on(layer_out, input_grad)
    dprob = last[:, 2 * width : 2 * width + 4] + last[:, 2 * width + 4 : 2 * width + 8]
    return (fwd_next, bwd_next, dprob)


def solution(mesh):
    return jax.shard_map(
        body,
        mesh=mesh,
        in_specs=(
            P(("segment", "expert"), None),
            P("segment", None),
            P("segment", None),
            P(("segment", "expert"), None),
            P("segment", None),
            P("segment", None),
            P(("segment", "expert"), None),
            P("segment", None, "expert"),
            P("segment", None, "expert"),
            P("segment", "expert", None),
        ),
        out_specs=(
            P(("segment", "expert"), None),
            P(("segment", "expert"), None),
            P(("segment", "expert"), None),
        ),
        check_vma=False,
    )
```

```python
import jax
import jax.numpy as jnp
from jax import lax
from jax.experimental import pallas as pl
from jax.experimental.pallas import tpu as pltpu
from jax.sharding import PartitionSpec as P

EXP_WIN = 8
SIDE = 4
LANES = 128
CHUNKS = 2
LOAD_CHUNKS = 4
LOADS = [(kind, c) for c in range(LOAD_CHUNKS) for kind in (0, 1)]
LOADS = LOADS + [(2, c) for c in range(LOAD_CHUNKS)]
STRIDE = {"z": 1, "x": 4, "y": 16}
F32 = jnp.float32
BF16 = jnp.bfloat16


def swap(value, along, by):
    length = lax.axis_size("expert")
    return lax.ppermute(
        value, "expert", [(i, i ^ (by * STRIDE[along])) for i in range(length)]
    )


def passed_along(value, axis, by):
    length = lax.axis_size(axis)
    return lax.ppermute(value, axis, [(i, (i + by) % length) for i in range(length)])


def handed_on(forth, back):
    length = lax.axis_size("segment")
    even = lax.axis_index("segment") % 2 == 0
    near = [(i, i ^ 1) for i in range(length)]
    far = [(i, (i - 1 if i % 2 == 0 else i + 1) % length) for i in range(length)]
    got_far = lax.ppermute(jnp.where(even, back, forth), "segment", far)
    got_near = lax.ppermute(jnp.where(even, forth, back), "segment", near)
    return jnp.where(even, got_far, got_near), jnp.where(even, got_near, got_far)


def gathered(value, along):
    return jnp.concatenate([value] + [swap(value, along, j) for j in range(1, SIDE)], axis=0)


def relayed(value, along, earlier):
    one, three = swap(value, along, 1), swap(value, along, 3)
    low, high = halves(three, one, earlier)
    return [value, one, swap(low, along, 1), swap(high, along, 3), three]


def scattered(own, others, along):
    for j, block in enumerate(others, 1):
        own = own + swap(block, along, j).astype(F32)
    return own


def cut(value, sent_as):
    blocks = value.reshape(SIDE, value.shape[0] // SIDE, value.shape[1])
    return blocks[0], [blocks[j].astype(sent_as) for j in range(1, SIDE)]


def to_other_order(value):
    rows, width = value.shape
    parts = value.reshape(SIDE, SIDE, rows // SIDE // SIDE, width)
    return parts.transpose(1, 0, 2, 3).reshape(rows, width)


def blocks_swapped(value):
    size = value.shape[0] // SIDE // SIDE
    return jnp.concatenate(
        [
            value[(b * SIDE + a) * size : (b * SIDE + a + 1) * size]
            for a in range(SIDE)
            for b in range(SIDE)
        ],
        axis=0,
    )


def contract_last(left, right):
    return lax.dot_general(
        left, right, (((1,), (1,)), ((), ())), preferred_element_type=F32
    )


def dot(left, right):
    return jnp.dot(left, right, preferred_element_type=F32)


def columns(pieces, first, step):
    return jnp.concatenate([ref[:, first : first + step] for ref in pieces], axis=0)


def halves_kernel(three, one, _, __, low, high, sems):
    half = low.shape[0]
    copies = (
        pltpu.make_async_copy(three.at[pl.ds(0, half), :], low, sems.at[0]),
        pltpu.make_async_copy(one.at[pl.ds(half, half), :], high, sems.at[1]),
    )
    for copy in copies:
        copy.start()
    for copy in copies:
        copy.wait()


def halves(three, one, earlier):
    vmem, there = pl.BlockSpec(memory_space=pltpu.VMEM), pl.BlockSpec(memory_space=pl.ANY)
    rows, width = one.shape
    out = jax.ShapeDtypeStruct((rows // 2, width), one.dtype)
    return pl.pallas_call(
        halves_kernel,
        out_shape=(out, out),
        in_specs=[vmem, vmem, there, there],
        out_specs=(vmem, vmem),
        scratch_shapes=[pltpu.SemaphoreType.DMA((2,))],
        compiler_params=pltpu.CompilerParams(vmem_limit_bytes=16 * 2**20),
    )(three, one, *earlier)


def forward_kernel(*refs):
    parts, tab_ref, hbm = refs[:5], refs[5], refs[6:9]
    wg, wu, wd, gate_b, up_b = refs[9:14]
    own, one_lo, one_hi, two_lo, two_hi, three_lo, three_hi, sems = refs[14:]
    width = wg.shape[0]
    step = width // LOAD_CHUNKS
    rows = parts[0].shape[0]
    count, half = SIDE * rows, rows // 2

    def load(kind, c):
        part = pl.ds(c * step, step)
        at = (slice(None), part) if kind == 2 else (part, slice(None))
        held = (wg, wu, wd)[kind]
        return pltpu.make_async_copy(hbm[kind].at[at], held.at[at], sems.at[kind, c])

    for kind, c in LOADS:
        load(kind, c).start()
    gate = up = gate_back = up_back = 0.0
    for c in range(LOAD_CHUNKS):
        at = c * step
        load(0, c).wait()
        load(1, c).wait()
        w_g, w_u = wg[at : at + step, :], wu[at : at + step, :]
        x = columns(parts, at, step)
        gate, up = gate + dot(x, w_g), up + dot(x, w_u)
        if c * 2 < LOAD_CHUNKS:
            x = columns(parts, width + at, step)
            gate_back, up_back = gate_back + dot(x, w_g), up_back + dot(x, w_u)
    gate_b[...] = blocks_swapped(gate_back)
    up_b[...] = blocks_swapped(up_back)

    hidden = (gate / (1.0 + jnp.exp(-gate)) * up).astype(BF16)
    weight = tab_ref[...]
    for c in range(LOAD_CHUNKS):
        load(2, c).wait()
        part = slice(c * step, (c + 1) * step)
        out = weight * dot(hidden, wd[:, part])
        own[:, part] = out[:rows]
        sent = out.astype(BF16)
        one_lo[:, part] = sent[rows : rows + half]
        one_hi[:, part] = out[rows + half : 2 * rows]
        two_lo[:, part] = sent[2 * rows : 2 * rows + half]
        two_hi[:, part] = sent[2 * rows + half : 3 * rows]
        three_lo[:, part] = out[3 * rows : 3 * rows + half]
        three_hi[:, part] = sent[3 * rows + half :]


def forward(parts, table, w_g, w_u, w_d):
    width, hidden = w_g.shape
    rows = parts[0].shape[0]
    half, count = rows // 2, SIDE * rows
    vmem = pl.BlockSpec(memory_space=pltpu.VMEM)
    out = jax.ShapeDtypeStruct
    return pl.pallas_call(
        forward_kernel,
        out_shape=(
            out(w_g.shape, BF16),
            out(w_u.shape, BF16),
            out(w_d.shape, BF16),
            out((count, hidden), F32),
            out((count, hidden), F32),
            out((rows, width), F32),
            out((half, width), BF16),
            out((half, width), F32),
            out((half, width), BF16),
            out((half, width), BF16),
            out((half, width), F32),
            out((half, width), BF16),
        ),
        in_specs=[vmem] * 6 + [pl.BlockSpec(memory_space=pl.ANY)] * 3,
        out_specs=(vmem,) * 12,
        scratch_shapes=[pltpu.SemaphoreType.DMA((3, LOAD_CHUNKS))],
        compiler_params=pltpu.CompilerParams(vmem_limit_bytes=36 * 2**20),
        cost_estimate=pl.CostEstimate(
            flops=2 * count * width * hidden * 4, bytes_accessed=6 * width * hidden, transcendentals=0
        ),
    )(*parts, table, w_g, w_u, w_d)


def backward_kernel(*refs):
    parts, (gate_b, up_b, tab_ref, wg, wu, wd) = refs[:5], refs[5:11]
    own, one, two, three, p_own = refs[11:]
    width = wg.shape[0]
    half_width, step = width // 2, width // CHUNKS
    rows = parts[0].shape[0]
    gate, up, back = gate_b[...], up_b[...], 0.0
    for c in range(CHUNKS):
        at = c * step
        back = back + contract_last(columns(parts, at, step), wd[:, at : at + step])
        if c * 2 >= CHUNKS:
            x = columns(parts, at + half_width, step)
            gate = gate + dot(x, wg[at : at + step, :])
            up = up + dot(x, wu[at : at + step, :])

    sig = 1.0 / (1.0 + jnp.exp(-gate))
    silu = gate * sig
    hidden = (silu * up).astype(BF16)
    inner = jnp.sum(hidden.astype(F32) * back, axis=-1, keepdims=True)
    grad_hidden = tab_ref[:, 8:9] * back
    dsilu = sig * (1.0 + gate * (1.0 - sig))
    grad_gate = (grad_hidden * up * dsilu).astype(BF16)
    grad_up = (grad_hidden * silu).astype(BF16)

    prob = tab_ref[:, :8] * inner
    p_own[...] = prob[:rows]
    top = prob.astype(BF16).astype(F32)
    lane = lax.broadcasted_iota(jnp.int32, prob.shape, 1)
    parts_of = jnp.where(lane < 4, top, prob - top).astype(BF16)
    for j, ref in enumerate((one, two, three), 1):
        ref[:, width:] = jnp.zeros((rows, LANES), BF16)
        ref[:, width : width + 8] = parts_of[j * rows : (j + 1) * rows]
    for c in range(CHUNKS):
        part = slice(c * step, (c + 1) * step)
        out = contract_last(grad_gate, wg[part, :]) + contract_last(grad_up, wu[part, :])
        own[:, part] = out[:rows]
        sent = out.astype(BF16)
        for j, ref in enumerate((one, two, three), 1):
            ref[:, part] = sent[j * rows : (j + 1) * rows]


def backward(parts, gate_b, up_b, table, w_g, w_u, w_d):
    width, hidden = w_g.shape
    rows = parts[0].shape[0]
    vmem = pl.BlockSpec(memory_space=pltpu.VMEM)
    out = jax.ShapeDtypeStruct
    sent = out((rows, width + LANES), BF16)
    return pl.pallas_call(
        backward_kernel,
        out_shape=(out((rows, width), F32), sent, sent, sent, out((rows, 8), F32)),
        in_specs=[vmem] * 11,
        out_specs=(vmem,) * 5,
        compiler_params=pltpu.CompilerParams(vmem_limit_bytes=24 * 2**20),
    )(*parts, gate_b, up_b, table, w_g, w_u, w_d)


def own_weight(ids, probs, expert_id):
    return jnp.sum(jnp.where(ids == expert_id, probs.astype(F32), 0.0), axis=-1)


def reordered(table, order):
    hit = order[:, None] == jnp.arange(table.shape[0], dtype=jnp.int32)[None, :]
    return jnp.sum(jnp.where(hit[:, :, None], table[None, :, :], 0.0), axis=1)


def body(x_fwd, ids_fwd, probs_fwd, x_bwd, ids_bwd, probs_bwd, grad_out, w_gate, w_up, w_down):
    width = x_fwd.shape[1]
    half = width // 2
    me = lax.axis_index("expert")
    expert_id = me // (lax.axis_size("expert") // EXP_WIN)

    spot = jnp.arange(SIDE**3 * 2, dtype=jnp.int32)
    order_a = ((spot // 2) ^ me) * 2 + spot % 2
    order_b = to_other_order(order_a[:, None])[:, 0]
    weight_f = own_weight(ids_fwd, probs_fwd, expert_id)
    weight_b = own_weight(ids_bwd, probs_bwd, expert_id)
    mine_b = (ids_bwd == expert_id).astype(F32)
    tab_f = reordered(weight_f[:, None], order_a)
    tab_b = reordered(jnp.concatenate([mine_b, mine_b, weight_b[:, None]], axis=1), order_b)
    tables = tab_f, tab_b

    first = jnp.concatenate([x_fwd, x_bwd[:, :half], grad_out, x_bwd[:, half:]], axis=1)
    lines = gathered(first, "z")
    a_part, b_part = lines[:, : width + half], lines[:, width + half :]
    a_parts = relayed(gathered(a_part, "x"), "y", tables)
    b_parts = relayed(gathered(b_part, "y"), "x", tables)

    (
        w_g, w_u, w_d, gate_b, up_b,
        f_own, f_one_lo, f_one_hi, f_two_lo, f_two_hi, f_three_lo, f_three_hi,
    ) = forward(a_parts, tab_f, w_gate[0], w_up[0], w_down[0])
    b_own, b_one, b_two, b_three, p_own = backward(b_parts, gate_b, up_b, tab_b, w_g, w_u, w_d)

    f_three_lo = (f_three_lo + swap(f_two_lo, "y", 1).astype(F32)).astype(BF16)
    f_one_hi = (f_one_hi + swap(f_two_hi, "y", 3).astype(F32)).astype(BF16)
    sum_f = (
        f_own
        + swap(jnp.concatenate([f_one_lo, f_one_hi], axis=0), "y", 1).astype(F32)
        + swap(jnp.concatenate([f_three_lo, f_three_hi], axis=0), "y", 3).astype(F32)
    )
    sum_b, sum_p = b_own, p_own[:, :4]
    for j, block in enumerate((b_one, b_two, b_three), 1):
        got = swap(block, "x", j).astype(F32)
        sum_b = sum_b + got[:, :width]
        sum_p = sum_p + got[:, width : width + 4] + got[:, width + 4 : width + 8]

    sum_f = scattered(*cut(sum_f, BF16), "x")
    top = lax.reduce_precision(sum_p, 8, 7)
    coded = jnp.pad(jnp.concatenate([top, sum_p - top], axis=1), ((0, 0), (0, LANES - 8)))
    both = scattered(*cut(jnp.concatenate([sum_b, coded], axis=1), BF16), "y")
    sum_b, coded = both[:, :width], both[:, width:]
    last = scattered(*cut(jnp.concatenate([sum_f, sum_b, coded], axis=1), F32), "z")

    layer_out = (x_fwd.astype(F32) + last[:, :width]).astype(BF16)
    input_grad = (grad_out.astype(F32) + last[:, width : 2 * width]).astype(BF16)
    fwd_next, bwd_next = handed_on(layer_out, input_grad)
    dprob = last[:, 2 * width : 2 * width + 4] + last[:, 2 * width + 4 : 2 * width + 8]
    return (fwd_next, bwd_next, dprob)


def solution(mesh):
    return jax.shard_map(
        body,
        mesh=mesh,
        in_specs=(
            P(("segment", "expert"), None),
            P("segment", None),
            P("segment", None),
            P(("segment", "expert"), None),
            P("segment", None),
            P("segment", None),
            P(("segment", "expert"), None),
            P("segment", None, "expert"),
            P("segment", None, "expert"),
            P("segment", "expert", None),
        ),
        out_specs=(
            P(("segment", "expert"), None),
            P(("segment", "expert"), None),
            P(("segment", "expert"), None),
        ),
        check_vma=False,
    )
```
